512 devices in a mesh: node: 16 (over x, z_hi), local: 8 (over y, core), edata: 4 (over z_lo).
Axes of the slice: x: 4, y: 4, z: 16 (z_hi: 4, z_lo: 4; z = z_hi * 4 + z_lo), core: 2. Of those that a mesh axis runs over, the one named last changes fastest.
Arguments:
- tokens: bfloat16 [32768, 4096], P(('node', 'local'), 'edata'), may hold values from -6 to 6
- grad_out: bfloat16 [32768, 4096], P(('node', 'local'), 'edata'), may hold values from -0.59765625 to 0.59765625
- routes: int32 [32768, 2], P(('node', 'local')), may hold values from 0 to 63, all different within a row
- gates: bfloat16 [32768, 2], P(('node', 'local')), may hold values from 0.099609375 to 1
- w_in: bfloat16 [4096, 32768], P('edata', ('node', 'local')), may hold values from -0.09375 to 0.09375
- w_out: bfloat16 [32768, 4096], P(('node', 'local'), 'edata'), may hold values from -0.09375 to 0.09375
Outputs:
- grad_tokens: bfloat16 [32768, 4096], P(('node', 'local'), 'edata')
- grad_gates: float32 [32768, 2], P(('node', 'local'))
- grad_w_in: float32 [4096, 32768], P('edata', ('node', 'local'))
- grad_w_out: float32 [32768, 4096], P(('node', 'local'), 'edata')
The draws below stay inside these ranges and needn't reach their ends.
Inputs may be any that keep to these rules, and one draw needn't show every extreme that they name: `routes`: each token names two different experts.
All inputs are finite; a program needn't handle non-finite values.
Results may differ from the reference program's by a relative error of at most 0.0049.
Values may be sent and summed in bfloat16 or wider, within the bound.
A program may use at most 64 MiB of HBM per device.

```python
import jax
import jax.numpy as jnp
from jax import lax

D = 4096
EXPERTS = 64
WINDOW = 2
TOK_DEV = 256
FFW = 16384
CAP = 8
TOKENS = 32768
N_NODE = 16
N_LOCAL = 8


def level_of(own_key, extent, pieces, smallest, high):
    def one(dim, blocks):
        draws = jax.random.uniform(jax.random.fold_in(jax.random.fold_in(own_key, 6), dim), (blocks,), jnp.float32, smallest / len(pieces), high / len(pieces))
        return jnp.repeat(jnp.exp(draws), extent[dim] // blocks).reshape((-1,) + (1,) * (len(extent) - dim - 1))

    factor_of = one(*pieces[0])
    for cut in pieces[1:]:
        factor_of = factor_of * one(*cut)
    return factor_of


def picks_of(own_key, rows, amount, top, lift):
    ranking = jax.random.permutation(jax.random.fold_in(own_key, 1), amount)
    boost = ranking
    for power in range(3):
        boost = boost * boost // amount
    boost = boost * lift // amount
    tickets = jax.random.randint(jax.random.fold_in(own_key, 2), (rows, amount), 0, 4096) + boost
    fixed_rows = jax.random.permutation(jax.random.fold_in(own_key, 3), rows)[jnp.arange(amount) % rows]
    tickets = jnp.where(jnp.arange(rows)[:, None] == fixed_rows[None, :], 1 << 14, tickets)
    priority = tickets * amount + jnp.arange(amount)
    return lax.top_k(priority.astype(jnp.int32), top)[1].astype(jnp.int32)


def scatter_about(stream_key, dims, deviation, most, cuts=(), kind=jnp.bfloat16):
    result = deviation * jax.random.normal(stream_key, dims, jnp.float32)
    if cuts:
        result = result * level_of(stream_key, dims, cuts, -0.22, 0.18)
    return jnp.clip(result, -most, most).astype(kind)


def setup_inputs(seed: int = 0) -> dict:
    key_of = jax.random.split(jax.random.key(seed), 7)
    tokens = scatter_about(key_of[0], (TOKENS, D), 1.0, 6.0, ((0, 128), (1, 4)))
    grad_out = scatter_about(key_of[1], (TOKENS, D), 0.1, 0.59765625, ((0, 128), (1, 4)))
    routes = picks_of(key_of[2], TOKENS, EXPERTS, 2, 0)
    gates = jnp.clip(0.099609375 + 0.9003906 * jax.random.uniform(key_of[3], (TOKENS, 2), jnp.float32) ** level_of(key_of[3], (TOKENS, 2), ((0, 128),), -0.2, 0.2), 0.099609375, 1.0).astype(jnp.bfloat16)
    w_in = scatter_about(key_of[4], (D, WINDOW * FFW), D ** -0.5, 0.09375, ((0, 4), (1, 128)))
    w_out = scatter_about(key_of[5], (WINDOW * FFW, D), D ** -0.5, 0.09375, ((0, 128), (1, 4)))
    return dict(tokens=tokens, grad_out=grad_out, routes=routes, gates=gates, w_in=w_in, w_out=w_out)


def gelu_pair(pre_act):
    coefficient = 0.7978845608028654
    inner_arg = coefficient * (pre_act + 0.044715 * pre_act * pre_act * pre_act)
    tanh_val = jnp.tanh(inner_arg)
    activation = 0.5 * pre_act * (1.0 + tanh_val)
    slopes = 0.5 * (1.0 + tanh_val) + 0.5 * pre_act * (1.0 - tanh_val * tanh_val) * coefficient * (1.0 + 3.0 * 0.044715 * pre_act * pre_act)
    return activation, slopes


def reference(tokens, grad_out, routes, gates, w_in, w_out):
    groups = N_NODE * N_LOCAL
    pairs = routes.reshape(groups, TOK_DEV * 2)
    onehot = (pairs[:, :, None] == jnp.arange(WINDOW, dtype=jnp.int32)[None, None, :]).astype(jnp.int32)
    before = jnp.cumsum(onehot, axis=1) - onehot
    position = jnp.sum(before * onehot, axis=2).astype(jnp.int32)
    live_pair = (pairs < WINDOW) & (position < CAP)
    slot_index = jnp.where(live_pair, pairs * CAP + position, -1).astype(jnp.int32)
    matches = slot_index[:, :, None] == jnp.arange(WINDOW * CAP, dtype=jnp.int32)[None, None, :]
    token_ids = jnp.arange(TOK_DEV * 2, dtype=jnp.int32) // 2
    token_of = jnp.sum(jnp.where(matches, token_ids[None, :, None], 0), axis=1).astype(jnp.int32)
    filled = jnp.any(matches, axis=1)
    gate_pairs = gates.reshape(groups, TOK_DEV * 2).astype(jnp.float32)
    gate_of = jnp.sum(jnp.where(matches, gate_pairs[:, :, None], jnp.zeros((), jnp.float32)), axis=1)
    group_base = (jnp.arange(groups, dtype=jnp.int32) * TOK_DEV)[:, None]
    in_grads = []
    out_grads = []
    slot_grads = []
    gate_parts = []
    for expert in range(WINDOW):
        local_ids = token_of[:, expert * CAP:(expert + 1) * CAP]
        live_rows = filled[:, expert * CAP:(expert + 1) * CAP].reshape(-1)
        gate_rows = gate_of[:, expert * CAP:(expert + 1) * CAP].reshape(-1)
        row_ids = (group_base + local_ids).reshape(-1).astype(jnp.int32)
        x_rows = jnp.where(live_rows[:, None], tokens[row_ids], jnp.zeros((), tokens.dtype))
        dy_rows = jnp.where(live_rows[:, None], grad_out[row_ids], jnp.zeros((), grad_out.dtype))
        w_in_e = w_in[:, expert * FFW:(expert + 1) * FFW]
        w_out_e = w_out[expert * FFW:(expert + 1) * FFW, :]
        pre_act = jnp.dot(x_rows, w_in_e, preferred_element_type=jnp.float32)
        back_grad = jnp.dot(dy_rows, w_out_e.T, preferred_element_type=jnp.float32)
        activation, slopes = gelu_pair(pre_act)
        scaled = (gate_rows[:, None] * activation).astype(jnp.bfloat16)
        out_grads.append(jnp.dot(scaled.T, dy_rows, preferred_element_type=jnp.float32))
        pre_grad = (gate_rows[:, None] * back_grad * slopes).astype(jnp.bfloat16)
        in_grads.append(jnp.dot(x_rows.T, pre_grad, preferred_element_type=jnp.float32))
        slot_grads.append(jnp.dot(pre_grad, w_in_e.T, preferred_element_type=jnp.float32))
        gate_parts.append(jnp.sum(activation * back_grad, axis=1))
    grad_w_in = jnp.concatenate(in_grads, axis=1)
    grad_w_out = jnp.concatenate(out_grads, axis=0)
    slot_flat = jnp.concatenate(slot_grads, axis=0)
    gate_flat = jnp.concatenate(gate_parts, axis=0)
    safe_expert = jnp.where(live_pair, pairs, 0)
    safe_pos = jnp.where(live_pair, position, 0)
    index = ((safe_expert * groups + jnp.arange(groups, dtype=jnp.int32)[:, None]) * CAP + safe_pos).reshape(-1).astype(jnp.int32)
    picked = slot_flat[index].reshape(groups * TOK_DEV, 2, tokens.shape[1])
    keep_pair = live_pair.reshape(groups * TOK_DEV, 2)
    grad_tokens = jnp.sum(jnp.where(keep_pair[:, :, None], picked, jnp.zeros((), picked.dtype)), axis=1).astype(jnp.bfloat16)
    grad_gates = jnp.where(keep_pair, gate_flat[index].reshape(groups * TOK_DEV, 2), jnp.zeros((), gate_flat.dtype))
    return grad_tokens, grad_gates, grad_w_in, grad_w_out
```

```python
import functools

import jax
import jax.numpy as jnp
from jax import lax
from jax.experimental import pallas as pl
from jax.experimental.pallas import tpu as pltpu
from jax.sharding import PartitionSpec as P

MESH = pl.DeviceIdType.MESH
BF, F32 = jnp.bfloat16, jnp.float32
WINDOW = 2
CAP = 8
LANES = 128
X_CHIPS, ZH_CHIPS = 4, 4


def gelu_pair(pre):
    coefficient = 0.7978845608028654
    tanh_val = jnp.tanh(coefficient * (pre + 0.044715 * pre * pre * pre))
    activation = 0.5 * pre * (1.0 + tanh_val)
    slopes = 0.5 * (1.0 + tanh_val) + 0.5 * pre * (1.0 - tanh_val * tanh_val) * coefficient * (
        1.0 + 3.0 * 0.044715 * pre * pre
    )
    return activation, slopes


def split(value):
    high = value.astype(BF)
    return high, (value - high.astype(F32)).astype(BF)


def dot_nt(a, b):
    return lax.dot_general(a, b, (((1,), (1,)), ((), ())), preferred_element_type=F32)


def dot_tn(a, b):
    return lax.dot_general(a, b, (((0,), (0,)), ((), ())), preferred_element_type=F32)


def wait_for(ref, sem):
    pltpu.make_async_copy(ref, ref, sem).wait()


def kernel(
    dims,
    tokens, grad_out, routes, gates, w_in, w_out,
    o_tokens, o_gates, o_w_in, o_w_out,
    zbuf, rows, xa, dya, part, rs_out, rs_in, res, res_sib, w_sib, dpa, sca, cs, cr, zs, zr, own,
    z_s, z_r, xy_s, xy_r, sib_s, sib_r, rs_s, rs_r, ag_s, ag_r, ds_s, ds_r, c_s, c_r, zc_s, zc_r, w_s, w_r,
):
    nx, nzh, ny, nzl = dims
    units = nx * ny
    half = units // 2
    hr = half * CAP
    n_half = 2 * nzh
    tok, fe = tokens.shape
    hid = w_in.shape[1]
    fh = fe // 2
    lat = 2 * (nzl - 1)
    offsets = [0] + [o for o in range(1, nzh) if o != nzh // 2] + ([nzh // 2] if nzh > 1 else [])

    node, local, zl = lax.axis_index("node"), lax.axis_index("local"), lax.axis_index("edata")
    x, zh, y, c = node // nzh, node % nzh, local // 2, local % 2
    me = y * nx + x
    sibling = (node, y * 2 + 1 - c, zl)

    def at_unit(u):
        return ((u % nx) * nzh + zh, (u // nx) * 2 + c, zl)

    def at_zh(other):
        return (x * nzh + other, local, zl)

    def offset_of(i):
        if nzh == 4:
            return jnp.where(i == 2, 3, jnp.where(i == 3, 2, i))
        return i

    pos = (nzl - 1 - zl, zl)
    ahead = (zl - 1, zl + 1)
    behind = (zl + 1, zl - 1)

    def remote(src, dst, send_sem, recv_sem, device):
        return pltpu.make_async_remote_copy(
            src_ref=src, dst_ref=dst, send_sem=send_sem, recv_sem=recv_sem, device_id=device, device_id_type=MESH
        )

    barrier = pltpu.get_barrier_semaphore()

    def greet(device):
        pl.semaphore_signal(barrier, inc=1, device_id=device, device_id_type=MESH)

    greet(sibling)
    for o in range(1, nzh):
        greet(at_zh((zh + o) % nzh))

    @pl.loop(1, units)
    def _(d):
        greet(at_unit((me + d) % units))

    @pl.when(zl > 0)
    def _():
        greet((node, local, zl - 1))

    @pl.when(zl < nzl - 1)
    def _():
        greet((node, local, zl + 1))

    lane = lax.broadcasted_iota(jnp.int32, (tok, LANES), 1)
    expert_of, place_of = (lane // CAP) % WINDOW, lane % CAP
    r0, r1 = routes[:, 0:1], routes[:, 1:2]
    g0, g1 = gates[:, 0:1].astype(F32), gates[:, 1:2].astype(F32)
    named = (r0 == expert_of) | (r1 == expert_of)
    earlier = lax.broadcasted_iota(jnp.int32, (tok, tok), 1) < lax.broadcasted_iota(jnp.int32, (tok, tok), 0)
    position = jnp.dot(
        jnp.where(earlier, 1.0, 0.0).astype(BF), jnp.where(named, 1.0, 0.0).astype(BF), preferred_element_type=F32
    )
    taken = named & (position == place_of.astype(F32)) & (lane < 3 * WINDOW * CAP)
    hot = jnp.where(taken, 1.0, 0.0).astype(BF)
    send_x, send_dy = dot_tn(hot, tokens[...]), dot_tn(hot, grad_out[...])
    for e in range(WINDOW):
        gate_e = jnp.where(r0 == e, g0, 0.0) + jnp.where(r1 == e, g1, 0.0)
        send_g = dot_tn(hot, jnp.broadcast_to(gate_e, (tok, LANES)).astype(BF))
        mine = slice(e * CAP, (e + 1) * CAP)
        zbuf[0, e, :, :fe] = jnp.concatenate([send_x[mine], send_dy[mine]], axis=0).astype(BF)
        zbuf[0, e, :, fe:] = jnp.concatenate([send_g[mine], send_g[mine]], axis=0).astype(BF)

    greeted = 1 + (nzh - 1) + (units - 1) + jnp.where(zl > 0, 1, 0) + jnp.where(zl < nzl - 1, 1, 0)
    pl.semaphore_wait(barrier, greeted)

    def dispatch(i):
        @pl.loop(0, units)
        def _(d):
            u = (me + d) % units
            src = zbuf.at[i, (u % nx) // (nx // 2)]
            dst = rows.at[i, c, me]

            @pl.when(d > 0)
            def _():
                remote(src, dst, xy_s.at[i], xy_r.at[i], at_unit(u)).start()

            @pl.when(d == 0)
            def _():
                pltpu.make_async_copy(src, dst, xy_r.at[i]).start()

    dispatch(0)
    for i in range(1, nzh):
        remote(zbuf.at[0], zbuf.at[i], z_s.at[i], z_r.at[i], at_zh((zh + nzh - offsets[i]) % nzh)).start()
    remote(w_in, w_sib, w_s, w_r, sibling).start()

    def pass_on(h, t, pre, back):
        high, low = split(pre)
        rs_out[h, t, :, 0:hid] = high
        rs_out[h, t, :, hid : 2 * hid] = low
        rs_out[h, t, :, 2 * hid :] = back.astype(BF)
        remote(
            rs_out.at[h, t], rs_in.at[h, t], rs_s.at[h], rs_r.at[h, t], (node, local, ahead[h])
        ).start()

    def send_back(h, t):
        remote(
            res.at[h, t], res.at[h, t], ag_s.at[h], ag_r.at[h, t], (node, local, behind[h])
        ).start()

    def partial_products(t):
        i, j = t // 2, t % 2
        parity = (c + j) % 2

        @pl.when(j == 0)
        def _():
            wait_for(rows.at[i, c], xy_r.at[i])
            remote(rows.at[i, c], rows.at[i, c], sib_s.at[i], sib_r.at[i], sibling).start()

        @pl.when(j == 1)
        def _():
            wait_for(rows.at[i, 1 - c], sib_r.at[i])

        for q in range(half):
            a = rows[i, parity, 2 * q, :, :fe].astype(F32)
            b = rows[i, parity, 2 * q + 1, :, :fe].astype(F32)
            xa[t, q * 16 : (q + 1) * 16, :] = jnp.concatenate([a[:CAP], b[:CAP]], axis=0).astype(BF)
            dya[t, q * 16 : (q + 1) * 16, :] = jnp.concatenate([a[CAP:], b[CAP:]], axis=0).astype(BF)
        part[t, :, :hid] = jnp.dot(xa[t], w_in[...], preferred_element_type=F32)
        part[t, :, hid:] = dot_nt(dya[t], w_out[...])
        for h in range(2):

            @pl.when(pos[h] == 0)
            def _():
                mine = slice(h * hr, (h + 1) * hr)
                pass_on(h, t, part[t, mine, :hid], part[t, mine, hid:])

    def sum_step(h, t):
        wait_for(rs_in.at[h, t], rs_r.at[h, t])
        mine = slice(h * hr, (h + 1) * hr)
        came = rs_in[h, t].astype(F32)
        pre = (came[:, :hid] + came[:, hid : 2 * hid]) + part[t, mine, :hid]
        back = came[:, 2 * hid :] + part[t, mine, hid:]

        @pl.when(pos[h] < nzl - 1)
        def _():
            pass_on(h, t, pre, back)

        @pl.when(pos[h] == nzl - 1)
        def _():
            i, parity = t // 2, (c + t % 2) % 2
            gate = rows[i, parity, h * half : (h + 1) * half, :, fe:].astype(F32)[:, :CAP]
            gate = gate.reshape(hr, LANES)
            gate = jnp.concatenate([gate] * (hid // LANES), axis=1)
            activation, slopes = gelu_pair(pre)
            res[h, t, :hr, :] = (gate * back * slopes).astype(BF)
            res[h, t, hr : 2 * hr, :] = (gate * activation).astype(BF)
            sums = jnp.sum(activation * back, axis=1, keepdims=True)
            small_lane = lax.broadcasted_iota(jnp.int32, (CAP, LANES), 1)
            packed = jnp.zeros((CAP, LANES), F32)
            for u in range(half):
                packed = jnp.where(small_lane == h * half + u, sums[u * CAP : (u + 1) * CAP], packed)
            high = packed.astype(BF).astype(F32)
            both = jnp.concatenate([high, packed - high], axis=0)
            both = jnp.concatenate([both] * (hid // LANES), axis=1)
            res[h, t, 2 * hr :, :] = both.astype(BF)
            send_back(h, t)

    def back_step(h, t):
        wait_for(res.at[h, t], ag_r.at[h, t])

        @pl.when(pos[h] > 0)
        def _():
            send_back(h, t)

    def keep(t):
        for h in range(2):
            mine = pl.ds(pl.multiple_of(t * 2 * hr + h * hr, hr), hr)
            dpa[mine, :] = res[h, t, :hr, :]
            sca[mine, :] = res[h, t, hr : 2 * hr, :]

    def to_sibling(i):
        for h in range(2):
            remote(res.at[h, 2 * i + 1], res_sib.at[i, h], ds_s.at[i, h], ds_r.at[i, h], sibling).start()

    def combine(i):
        t = 2 * i
        for h in range(2):
            wait_for(res_sib.at[i, h], ds_r.at[i, h])

        @pl.when(i == 0)
        def _():
            wait_for(w_sib, w_r)

        d_own = jnp.concatenate([res[0, t, :hr, :], res[1, t, :hr, :]], axis=0)
        d_sib = jnp.concatenate([res_sib[i, 0, :hr, :], res_sib[i, 1, :hr, :]], axis=0)
        total = dot_nt(d_own, w_in[...]) + dot_nt(d_sib, w_sib[...])
        packed = jnp.zeros((CAP, LANES), F32)
        for h in range(2):
            for ref in (res[h, t, 2 * hr :, :LANES], res_sib[i, h, 2 * hr :, :LANES]):
                both = ref.astype(F32)
                packed = packed + (both[:CAP] + both[CAP:])
        small_lane = lax.broadcasted_iota(jnp.int32, (CAP, LANES), 1)
        for u in range(units):
            mine = total[u * CAP : (u + 1) * CAP]
            cs[i, u, :, :fh] = jnp.concatenate([mine[:, :fh], mine[:, fh:]], axis=0).astype(BF)
            gate = jnp.sum(jnp.where(small_lane == u, packed, 0.0), axis=1, keepdims=True)
            gate = jnp.broadcast_to(gate, (CAP, LANES))
            high = gate.astype(BF).astype(F32)
            cs[i, u, :, fh:] = jnp.concatenate([high, gate - high], axis=0).astype(BF)

        @pl.loop(0, units)
        def _(d):
            u = (me + d) % units

            @pl.when(d > 0)
            def _():
                remote(cs.at[i, u], cr.at[i, me], c_s.at[i], c_r.at[i], at_unit(u)).start()

            @pl.when(d == 0)
            def _():
                pltpu.make_async_copy(cs.at[i, u], cr.at[i, me], c_r.at[i]).start()

    def sum_units(i):
        wait_for(cr.at[i], c_r.at[i])
        for e in range(WINDOW):
            total = jnp.zeros((2 * CAP, fh + LANES), F32)
            for yy in range(ny):
                for xx in range(e * (nx // 2), (e + 1) * (nx // 2)):
                    total = total + cr[i, yy * nx + xx].astype(F32)

            @pl.when(i == 0)
            def _():
                own[e] = total

            @pl.when(i > 0)
            def _():
                gate = total[:CAP, fh:] + total[CAP:, fh:]
                high = gate.astype(BF).astype(F32)
                zs[i, e, :, :fh] = total[:, :fh].astype(BF)
                zs[i, e, :, fh:] = jnp.concatenate([high, gate - high], axis=0).astype(BF)

        @pl.when(i > 0)
        def _():
            remote(
                zs.at[i], zr.at[i], zc_s.at[i], zc_r.at[i], at_zh((zh + offset_of(i)) % nzh)
            ).start()

    slots = 2 * (nzh - 1) + 2 + lat + 1

    @pl.loop(0, slots)
    def _(s):
        for h in range(2):
            t = s - lat + pos[h]

            @pl.when((pos[h] < nzl - 1) & (t >= 0) & (t < n_half))
            def _():
                back_step(h, t)

        for h in range(2):
            t = s - pos[h]

            @pl.when((pos[h] > 0) & (t >= 0) & (t < n_half))
            def _():
                sum_step(h, t)

        @pl.when(s < n_half)
        def _():
            partial_products(s)

        @pl.when((s % 2 == 0) & (s // 2 + 1 < nzh))
        def _():
            i = s // 2 + 1
            wait_for(zbuf.at[i], z_r.at[i])
            dispatch(i)

        done = s - lat

        @pl.when((done >= 0) & (done < n_half))
        def _():
            keep(done)

            @pl.when(done % 2 == 1)
            def _():
                to_sibling(done // 2)

        @pl.when((done >= 2) & (done % 2 == 0))
        def _():
            combine(done // 2 - 1)

        @pl.when((done >= 4) & (done % 2 == 0))
        def _():
            sum_units(done // 2 - 2)

    tile = min(256, fe)

    @pl.loop(0, fe // tile)
    def _(m):
        cols = pl.ds(pl.multiple_of(m * tile, tile), tile)
        o_w_out[:, cols] = dot_tn(sca[...], dya[:, :, cols].reshape(n_half * 2 * hr, tile))

    sum_units(nzh - 1)

    @pl.loop(0, fe // tile)
    def _(m):
        cols = pl.ds(pl.multiple_of(m * tile, tile), tile)
        o_w_in[cols, :] = dot_tn(xa[:, :, cols].reshape(n_half * 2 * hr, tile), dpa[...])

    slot, gate_slot = [], []
    for i in range(1, nzh):
        wait_for(zr.at[i], zc_r.at[i])
    for e in range(WINDOW):
        total = own[e]
        for i in range(1, nzh):
            total = total + zr[i, e].astype(F32)
        slot.append(jnp.concatenate([total[:CAP, :fh], total[CAP:, :fh]], axis=1))
        gate_slot.append(total[:CAP, fh:] + total[CAP:, fh:])
    slot = jnp.concatenate(slot, axis=0)
    lane_half = lax.broadcasted_iota(jnp.int32, (CAP, LANES), 1) // (LANES // 2)
    gate_slot = jnp.concatenate([jnp.where(lane_half == e, gate_slot[e], 0.0) for e in range(WINDOW)], axis=0)

    def three(value):
        high = value.astype(BF).astype(F32)
        middle = (value - high).astype(BF).astype(F32)
        low = value - high - middle
        rest = jnp.zeros((LANES - 3 * WINDOW * CAP, value.shape[1]), F32)
        return jnp.concatenate([high, middle, low, rest], axis=0).astype(BF)

    o_tokens[...] = jnp.dot(hot, three(slot), preferred_element_type=F32).astype(BF)
    gate_rows = jnp.dot(hot, three(gate_slot), preferred_element_type=F32)
    first, second = gate_rows[:, 0:1], gate_rows[:, LANES // 2 : LANES // 2 + 1]
    for k, r in enumerate((r0, r1)):
        o_gates[:, k : k + 1] = jnp.where(r == 0, first, jnp.where(r == 1, second, 0.0))

    for i in range(1, nzh):
        wait_for(zbuf.at[0], z_s.at[i])
        wait_for(zs.at[i], zc_s.at[i])
    for i in range(nzh):
        wait_for(rows.at[i, 0, pl.ds(0, units - 1)], xy_s.at[i])
        wait_for(rows.at[i, 0], sib_s.at[i])
        wait_for(cs.at[i, pl.ds(0, units - 1)], c_s.at[i])
        for h in range(2):
            wait_for(res_sib.at[i, h], ds_s.at[i, h])
    wait_for(w_sib, w_s)
    for h in range(2):

        @pl.when(pos[h] < nzl - 1)
        def _():
            wait_for(rs_out.at[h], rs_s.at[h])

        @pl.when(pos[h] > 0)
        def _():
            wait_for(res.at[h], ag_s.at[h])


def body(dims, tokens, grad_out, routes, gates, w_in, w_out):
    nx, nzh, ny, nzl = dims
    units = nx * ny
    hr = units * CAP // 2
    n_half = 2 * nzh
    tok, fe = tokens.shape
    hid = w_in.shape[1]
    all_rows = n_half * 2 * hr
    vmem = pl.BlockSpec(memory_space=pltpu.VMEM)
    dma = pltpu.SemaphoreType.DMA
    return pl.pallas_call(
        functools.partial(kernel, dims),
        out_shape=(
            jax.ShapeDtypeStruct((tok, fe), BF),
            jax.ShapeDtypeStruct((tok, 2), F32),
            jax.ShapeDtypeStruct((fe, hid), F32),
            jax.ShapeDtypeStruct((hid, fe), F32),
        ),
        in_specs=[vmem] * 6,
        out_specs=(vmem,) * 4,
        scratch_shapes=[
            pltpu.VMEM((nzh, WINDOW, 2 * CAP, fe + LANES), BF),
            pltpu.VMEM((nzh, 2, units, 2 * CAP, fe + LANES), BF),
            pltpu.VMEM((n_half, 2 * hr, fe), BF),
            pltpu.VMEM((n_half, 2 * hr, fe), BF),
            pltpu.VMEM((n_half, 2 * hr, 2 * hid), F32),
            pltpu.VMEM((2, n_half, hr, 3 * hid), BF),
            pltpu.VMEM((2, n_half, hr, 3 * hid), BF),
            pltpu.VMEM((2, n_half, 2 * hr + 16, hid), BF),
            pltpu.VMEM((nzh, 2, 2 * hr + 16, hid), BF),
            pltpu.VMEM((fe, hid), BF),
            pltpu.VMEM((all_rows, hid), BF),
            pltpu.VMEM((all_rows, hid), BF),
            pltpu.VMEM((nzh, units, 2 * CAP, fe // 2 + LANES), BF),
            pltpu.VMEM((nzh, units, 2 * CAP, fe // 2 + LANES), BF),
            pltpu.VMEM((nzh, WINDOW, 2 * CAP, fe // 2 + LANES), BF),
            pltpu.VMEM((nzh, WINDOW, 2 * CAP, fe // 2 + LANES), BF),
            pltpu.VMEM((WINDOW, 2 * CAP, fe // 2 + LANES), F32),
            dma((nzh,)), dma((nzh,)),
            dma((nzh,)), dma((nzh,)),
            dma((nzh,)), dma((nzh,)),
            dma((2,)), dma((2, n_half)),
            dma((2,)), dma((2, n_half)),
            dma((nzh, 2)), dma((nzh, 2)),
            dma((nzh,)), dma((nzh,)),
            dma((nzh,)), dma((nzh,)),
            dma, dma,
        ],
        compiler_params=pltpu.CompilerParams(
            collective_id=0, has_side_effects=True, vmem_limit_bytes=56 * 1024 * 1024
        ),
    )(tokens, grad_out, routes, gates, w_in, w_out)


def solution(mesh):
    dims = (X_CHIPS, ZH_CHIPS, mesh.shape["local"] // 2, mesh.shape["edata"])
    in_specs = (
        P(("node", "local"), "edata"),
        P(("node", "local"), "edata"),
        P(("node", "local"), None),
        P(("node", "local"), None),
        P("edata", ("node", "local")),
        P(("node", "local"), "edata"),
    )
    out_specs = (
        P(("node", "local"), "edata"),
        P(("node", "local"), None),
        P("edata", ("node", "local")),
        P(("node", "local"), "edata"),
    )
    return jax.shard_map(
        functools.partial(body, dims), mesh=mesh, in_specs=in_specs, out_specs=out_specs, check_vma=False
    )
```

```python
import functools

import jax
import jax.numpy as jnp
from jax import lax
from jax.experimental import pallas as pl
from jax.experimental.pallas import tpu as pltpu
from jax.sharding import PartitionSpec as P

MESH = pl.DeviceIdType.MESH
BF, F32 = jnp.bfloat16, jnp.float32
WINDOW = 2
CAP = 8
LANES = 128
X_CHIPS, ZH_CHIPS = 4, 4
HOP = 2
OWN_LAST = False


def half_chunks(nzh):
    if OWN_LAST:
        return [(0, 0)] + [(i, j) for i in range(1, nzh) for j in range(2)] + [(0, 1)]
    return [(i, j) for i in range(nzh) for j in range(2)]


def pick(table, t):
    value = table[0]
    for k in range(1, len(table)):
        value = jnp.where(t == k, table[k], value)
    return value


def gelu_pair(pre):
    coefficient = 0.7978845608028654
    tanh_val = jnp.tanh(coefficient * (pre + 0.044715 * pre * pre * pre))
    activation = 0.5 * pre * (1.0 + tanh_val)
    slopes = 0.5 * (1.0 + tanh_val) + 0.5 * pre * (1.0 - tanh_val * tanh_val) * coefficient * (
        1.0 + 3.0 * 0.044715 * pre * pre
    )
    return activation, slopes


def split(value):
    high = value.astype(BF)
    return high, (value - high.astype(F32)).astype(BF)


def dot_nt(a, b):
    return lax.dot_general(a, b, (((1,), (1,)), ((), ())), preferred_element_type=F32)


def dot_tn(a, b):
    return lax.dot_general(a, b, (((0,), (0,)), ((), ())), preferred_element_type=F32)


def wait_for(ref, sem):
    pltpu.make_async_copy(ref, ref, sem).wait()


def kernel(
    dims,
    tokens_hbm, grad_out_hbm, routes, gates, w_in_hbm, w_out_hbm,
    o_tokens, o_gates, o_w_in, o_w_out,
    tokens, grad_out, w_in, w_out, zbuf, rows, xa, dya, part, rs_out, rs_in, res, res_sib, w_sib, dpa, sca, cs, cr, zs, zr, own,
    z_s, z_r, xy_s, xy_r, sib_s, sib_r, rs_s, rs_r, ag_s, ag_r, ds_s, ds_r, c_s, c_r, zc_s, zc_r, w_s, w_r, in_sem,
):
    nx, nzh, ny, nzl = dims
    units = nx * ny
    half = units // 2
    hr = half * CAP
    n_half = 2 * nzh
    tok, fe = tokens.shape
    hid = w_in.shape[1]
    fh = fe // 2
    lat = 2 * HOP * (nzl - 1)
    offsets = list(range(nzh))
    near = [1, 3] if nzh == 4 else list(range(1, nzh))
    far = 2 if nzh == 4 else None

    node, local, zl = lax.axis_index("node"), lax.axis_index("local"), lax.axis_index("edata")
    x, zh, y, c = node // nzh, node % nzh, local // 2, local % 2
    me = y * nx + x
    sibling = (node, y * 2 + 1 - c, zl)

    def at_unit(u):
        return ((u % nx) * nzh + zh, (u // nx) * 2 + c, zl)

    def at_zh(other):
        return (x * nzh + other, local, zl)

    order = half_chunks(nzh)
    ends = {i: order.index((i, 1)) for i in range(nzh)}

    def chunk_of(t):
        return pick([i for i, _ in order], t)

    def which_of(t):
        return pick([j for _, j in order], t)

    pos = (nzl - 1 - zl, zl)
    ahead = (zl - 1, zl + 1)
    behind = (zl + 1, zl - 1)

    def remote(src, dst, send_sem, recv_sem, device):
        return pltpu.make_async_remote_copy(
            src_ref=src, dst_ref=dst, send_sem=send_sem, recv_sem=recv_sem, device_id=device, device_id_type=MESH
        )

    loads = [
        pltpu.make_async_copy(src, dst, in_sem.at[n])
        for n, (src, dst) in enumerate(
            ((tokens_hbm, tokens), (grad_out_hbm, grad_out), (w_in_hbm, w_in), (w_out_hbm, w_out))
        )
    ]
    for load in loads:
        load.start()

    barrier = pltpu.get_barrier_semaphore()

    def greet(device):
        pl.semaphore_signal(barrier, inc=1, device_id=device, device_id_type=MESH)

    greet(sibling)
    for o in range(1, nzh):
        greet(at_zh((zh + o) % nzh))

    @pl.loop(1, units)
    def _(d):
        greet(at_unit((me + d) % units))

    @pl.when(zl > 0)
    def _():
        greet((node, local, zl - 1))

    @pl.when(zl < nzl - 1)
    def _():
        greet((node, local, zl + 1))

    slot_rows = 3 * WINDOW * CAP
    row = lax.broadcasted_iota(jnp.int32, (slot_rows, tok), 0)
    expert_of, place_of = (row // CAP) % WINDOW, row % CAP
    r0, r1 = routes[0:1, :], routes[1:2, :]
    g0, g1 = gates[0:1, :].astype(F32), gates[1:2, :].astype(F32)
    named = (r0 == expert_of) | (r1 == expert_of)
    earlier = lax.broadcasted_iota(jnp.int32, (tok, tok), 0) < lax.broadcasted_iota(jnp.int32, (tok, tok), 1)
    position = jnp.dot(
        jnp.where(named, 1.0, 0.0).astype(BF), jnp.where(earlier, 1.0, 0.0).astype(BF), preferred_element_type=F32
    )
    hot_f = jnp.where(named & (position == place_of.astype(F32)), 1.0, 0.0)
    hot = hot_f.astype(BF)
    send_g = jnp.sum(hot_f * jnp.where(r0 == expert_of, g0, g1), axis=1, keepdims=True)
    send_g = jnp.broadcast_to(send_g, (slot_rows, LANES))
    loads[0].wait()
    send_x = jnp.dot(hot, tokens[...], preferred_element_type=F32)
    loads[1].wait()
    send_dy = jnp.dot(hot, grad_out[...], preferred_element_type=F32)
    for e in range(WINDOW):
        mine = slice(e * CAP, (e + 1) * CAP)
        zbuf[0, e, :, :fe] = jnp.concatenate([send_x[mine], send_dy[mine]], axis=0).astype(BF)
        zbuf[0, e, :, fe:] = jnp.concatenate([send_g[mine], send_g[mine]], axis=0).astype(BF)

    greeted = 1 + (nzh - 1) + (units - 1) + jnp.where(zl > 0, 1, 0) + jnp.where(zl < nzl - 1, 1, 0)
    pl.semaphore_wait(barrier, greeted)

    def dispatch(i):
        @pl.loop(0, units)
        def _(d):
            u = (me + d) % units
            src = zbuf.at[i, (u % nx) // (nx // 2)]
            dst = rows.at[i, c, me]

            @pl.when(d > 0)
            def _():
                remote(src, dst, xy_s.at[i], xy_r.at[i], at_unit(u)).start()

            @pl.when(d == 0)
            def _():
                pltpu.make_async_copy(src, dst, xy_r.at[i]).start()

    for i in near:
        remote(zbuf.at[0], zbuf.at[i], z_s.at[i], z_r.at[i], at_zh((zh + nzh - offsets[i]) % nzh)).start()
    dispatch(0)
    loads[2].wait()
    remote(w_in, w_sib, w_s, w_r, sibling).start()
    loads[3].wait()

    def arrive(i):
        if far is None:
            wait_for(zbuf.at[i], z_r.at[i])
        else:

            @pl.when(i == 1)
            def _():
                for e, k in enumerate(near):
                    wait_for(zbuf.at[k], z_r.at[k])
                    remote(
                        zbuf.at[k, e], zbuf.at[far, e], z_s.at[nzh + e], z_r.at[nzh + e], at_zh((zh + nzh - k) % nzh)
                    ).start()

            @pl.when(i == far)
            def _():
                for e in range(WINDOW):
                    wait_for(zbuf.at[far, e], z_r.at[nzh + e])

    def pass_on(h, t, pre, back):
        high, low = split(pre)
        rs_out[h, t, :, 0:hid] = high
        rs_out[h, t, :, hid : 2 * hid] = low
        rs_out[h, t, :, 2 * hid :] = back.astype(BF)
        remote(
            rs_out.at[h, t], rs_in.at[h, t], rs_s.at[h], rs_r.at[h, t], (node, local, ahead[h])
        ).start()

    def send_back(h, t):
        remote(
            res.at[h, t], res.at[h, t], ag_s.at[h], ag_r.at[h, t], (node, local, behind[h])
        ).start()

    def partial_products(t):
        i, j = chunk_of(t), which_of(t)
        parity = (c + j) % 2

        @pl.when(j == 0)
        def _():
            wait_for(rows.at[i, c], xy_r.at[i])
            remote(rows.at[i, c], rows.at[i, c], sib_s.at[i], sib_r.at[i], sibling).start()

        @pl.when(j == 1)
        def _():
            wait_for(rows.at[i, 1 - c], sib_r.at[i])

        for q in range(half):
            a = rows[i, parity, 2 * q, :, :fe].astype(F32)
            b = rows[i, parity, 2 * q + 1, :, :fe].astype(F32)
            xa[t, q * 16 : (q + 1) * 16, :] = jnp.concatenate([a[:CAP], b[:CAP]], axis=0).astype(BF)
            dya[t, q * 16 : (q + 1) * 16, :] = jnp.concatenate([a[CAP:], b[CAP:]], axis=0).astype(BF)
        part[t, :, :hid] = jnp.dot(xa[t], w_in[...], preferred_element_type=F32)
        part[t, :, hid:] = dot_nt(dya[t], w_out[...])
        for h in range(2):

            @pl.when(pos[h] == 0)
            def _():
                mine = slice(h * hr, (h + 1) * hr)
                pass_on(h, t, part[t, mine, :hid], part[t, mine, hid:])

    def sum_step(h, t):
        wait_for(rs_in.at[h, t], rs_r.at[h, t])
        mine = slice(h * hr, (h + 1) * hr)
        came = rs_in[h, t].astype(F32)
        pre = (came[:, :hid] + came[:, hid : 2 * hid]) + part[t, mine, :hid]
        back = came[:, 2 * hid :] + part[t, mine, hid:]

        @pl.when(pos[h] < nzl - 1)
        def _():
            pass_on(h, t, pre, back)

        @pl.when(pos[h] == nzl - 1)
        def _():
            i, parity = chunk_of(t), (c + which_of(t)) % 2
            gate = rows[i, parity, h * half : (h + 1) * half, :, fe:].astype(F32)[:, :CAP]
            gate = gate.reshape(hr, LANES)
            gate = jnp.concatenate([gate] * (hid // LANES), axis=1)
            activation, slopes = gelu_pair(pre)
            res[h, t, :hr, :] = (gate * back * slopes).astype(BF)
            res[h, t, hr : 2 * hr, :] = (gate * activation).astype(BF)
            sums = jnp.sum(activation * back, axis=1, keepdims=True)
            small_lane = lax.broadcasted_iota(jnp.int32, (CAP, LANES), 1)
            packed = jnp.zeros((CAP, LANES), F32)
            for u in range(half):
                packed = jnp.where(small_lane == h * half + u, sums[u * CAP : (u + 1) * CAP], packed)
            high = packed.astype(BF).astype(F32)
            both = jnp.concatenate([high, packed - high], axis=0)
            both = jnp.concatenate([both] * (hid // LANES), axis=1)
            res[h, t, 2 * hr :, :] = both.astype(BF)
            send_back(h, t)

    def back_step(h, t):
        wait_for(res.at[h, t], ag_r.at[h, t])

        @pl.when(pos[h] > 0)
        def _():
            send_back(h, t)

    def keep(t):
        for h in range(2):
            mine = pl.ds(pl.multiple_of(t * 2 * hr + h * hr, hr), hr)
            dpa[mine, :] = res[h, t, :hr, :]
            sca[mine, :] = res[h, t, hr : 2 * hr, :]

    def to_sibling(i):
        for h in range(2):
            remote(res.at[h, pick([ends[k] for k in range(nzh)], i)], res_sib.at[i, h], ds_s.at[i, h], ds_r.at[i, h], sibling).start()

    def combine(i):
        t = pick([order.index((k, 0)) for k in range(nzh)], i)
        for h in range(2):
            wait_for(res_sib.at[i, h], ds_r.at[i, h])

        d_own = jnp.concatenate([res[0, t, :hr, :], res[1, t, :hr, :]], axis=0)
        d_sib = jnp.concatenate([res_sib[i, 0, :hr, :], res_sib[i, 1, :hr, :]], axis=0)
        total = dot_nt(d_own, w_in[...]) + dot_nt(d_sib, w_sib[...])
        packed = jnp.zeros((CAP, LANES), F32)
        for h in range(2):
            for ref in (res[h, t, 2 * hr :, :LANES], res_sib[i, h, 2 * hr :, :LANES]):
                both = ref.astype(F32)
                packed = packed + (both[:CAP] + both[CAP:])
        small_lane = lax.broadcasted_iota(jnp.int32, (CAP, LANES), 1)
        for u in range(units):
            mine = total[u * CAP : (u + 1) * CAP]
            cs[i, u, :, :fh] = jnp.concatenate([mine[:, :fh], mine[:, fh:]], axis=0).astype(BF)
            gate = jnp.sum(jnp.where(small_lane == u, packed, 0.0), axis=1, keepdims=True)
            gate = jnp.broadcast_to(gate, (CAP, LANES))
            high = gate.astype(BF).astype(F32)
            cs[i, u, :, fh:] = jnp.concatenate([high, gate - high], axis=0).astype(BF)

        @pl.loop(0, units)
        def _(d):
            u = (me + d) % units

            @pl.when(d > 0)
            def _():
                remote(cs.at[i, u], cr.at[i, me], c_s.at[i], c_r.at[i], at_unit(u)).start()

            @pl.when(d == 0)
            def _():
                pltpu.make_async_copy(cs.at[i, u], cr.at[i, me], c_r.at[i]).start()

    def sum_units(i):
        wait_for(cr.at[i], c_r.at[i])
        for e in range(WINDOW):
            total = jnp.zeros((2 * CAP, fh + LANES), F32)
            for yy in range(ny):
                for xx in range(e * (nx // 2), (e + 1) * (nx // 2)):
                    total = total + cr[i, yy * nx + xx].astype(F32)

            @pl.when(i == 0)
            def _():
                own[e] = total

            @pl.when(i > 0)
            def _():
                gate = total[:CAP, fh:] + total[CAP:, fh:]
                high = gate.astype(BF).astype(F32)
                zs[i, e, :, :fh] = total[:, :fh].astype(BF)
                zs[i, e, :, fh:] = jnp.concatenate([high, gate - high], axis=0).astype(BF)

        @pl.when(i > 0)
        def _():
            remote(
                zs.at[i], zr.at[i], zc_s.at[i], zc_r.at[i], at_zh((zh + pick(offsets, i)) % nzh)
            ).start()

    tile = min(256, fe)

    @pl.loop(0, n_half + lat)
    def _(s):
        @pl.when(s < n_half)
        def _():
            partial_products(s)

        for h in range(2):
            t = s - HOP * pos[h]

            @pl.when((pos[h] > 0) & (t >= 0) & (t < n_half))
            def _():
                sum_step(h, t)

        for h in range(2):
            t = s - lat + HOP * pos[h]

            @pl.when((pos[h] < nzl - 1) & (t >= 0) & (t < n_half))
            def _():
                back_step(h, t)

        @pl.when(s + 1 < nzh)
        def _():
            i = s + 1

            arrive(i)
            dispatch(i)

        done = s - lat

        @pl.when(done >= 0)
        def _():
            @pl.when(done == 0)
            def _():
                wait_for(w_sib, w_r)

            keep(done)

            @pl.when(which_of(done) == 1)
            def _():
                to_sibling(chunk_of(done))

        @pl.when((done >= 1) & (which_of(done - 1) == 1))
        def _():
            combine(chunk_of(done - 1))

        @pl.when((done >= 4) & (which_of(done - 4) == 1))
        def _():
            sum_units(chunk_of(done - 4))

    def finish_w_out(first, last):
        @pl.loop(first, last)
        def _(m):
            cols = pl.ds(pl.multiple_of(m * tile, tile), tile)
            o_w_out[:, cols] = dot_tn(sca[...], dya[:, :, cols].reshape(n_half * 2 * hr, tile))

    tiles = fe // tile
    finish_w_out(0, tiles // 2)
    combine(order[-1][0])
    late = [i for t, (i, j) in enumerate(order) if j == 1 and t >= n_half - 4]
    for i in late[:-1]:
        sum_units(i)
    finish_w_out(tiles // 2, tiles)
    sum_units(late[-1])

    @pl.loop(0, tiles)
    def _(m):
        cols = pl.ds(pl.multiple_of(m * tile, tile), tile)
        o_w_in[cols, :] = dot_tn(xa[:, :, cols].reshape(n_half * 2 * hr, tile), dpa[...])

    slot, gate_slot = [], []
    for i in range(1, nzh):
        wait_for(zr.at[i], zc_r.at[i])
    for e in range(WINDOW):
        total = own[e]
        for i in range(1, nzh):
            total = total + zr[i, e].astype(F32)
        slot.append(jnp.concatenate([total[:CAP, :fh], total[CAP:, :fh]], axis=1))
        gate_slot.append(total[:CAP, fh:] + total[CAP:, fh:])
    slot = jnp.concatenate(slot, axis=0)
    high = slot.astype(BF).astype(F32)
    middle = (slot - high).astype(BF).astype(F32)
    o_tokens[...] = dot_tn(hot, jnp.concatenate([high, middle, slot - high - middle], axis=0).astype(BF)).astype(BF)
    gate_slot = jnp.concatenate(gate_slot, axis=0)
    gate_slot = jnp.concatenate([gate_slot] * (tok // LANES), axis=1) * hot_f[: WINDOW * CAP]
    for k, r in enumerate((r0, r1)):
        kept = jnp.where(r == expert_of[: WINDOW * CAP], gate_slot, 0.0)
        o_gates[k : k + 1, :] = jnp.sum(kept, axis=0, keepdims=True)

    for i in range(1, nzh):
        wait_for(zs.at[i], zc_s.at[i])
    for i in near:
        wait_for(zbuf.at[0], z_s.at[i])
    if far is not None:
        for e in range(WINDOW):
            wait_for(zbuf.at[0, e], z_s.at[nzh + e])
    for i in range(nzh):
        wait_for(rows.at[i, 0, pl.ds(0, units - 1)], xy_s.at[i])
        wait_for(rows.at[i, 0], sib_s.at[i])
        wait_for(cs.at[i, pl.ds(0, units - 1)], c_s.at[i])
        for h in range(2):
            wait_for(res_sib.at[i, h], ds_s.at[i, h])
    wait_for(w_sib, w_s)
    for h in range(2):

        @pl.when(pos[h] < nzl - 1)
        def _():
            wait_for(rs_out.at[h], rs_s.at[h])

        @pl.when(pos[h] > 0)
        def _():
            wait_for(res.at[h], ag_s.at[h])


def body(dims, tokens, grad_out, routes, gates, w_in, w_out):
    nx, nzh, ny, nzl = dims
    units = nx * ny
    hr = units * CAP // 2
    n_half = 2 * nzh
    tok, fe = tokens.shape
    hid = w_in.shape[1]
    all_rows = n_half * 2 * hr
    vmem, hbm = pl.BlockSpec(memory_space=pltpu.VMEM), pl.BlockSpec(memory_space=pltpu.HBM)
    dma = pltpu.SemaphoreType.DMA
    grad_tokens, grad_gates, grad_w_in, grad_w_out = pl.pallas_call(
        functools.partial(kernel, dims),
        out_shape=(
            pltpu.VMEM((tok, fe), BF),
            pltpu.VMEM((2, tok), F32),
            pltpu.VMEM((fe, hid), F32),
            pltpu.VMEM((hid, fe), F32),
        ),
        in_specs=[hbm, hbm, vmem, vmem, hbm, hbm],
        out_specs=(vmem,) * 4,
        scratch_shapes=[
            pltpu.VMEM((tok, fe), BF),
            pltpu.VMEM((tok, fe), BF),
            pltpu.VMEM((fe, hid), BF),
            pltpu.VMEM((hid, fe), BF),
            pltpu.VMEM((nzh, WINDOW, 2 * CAP, fe + LANES), BF),
            pltpu.VMEM((nzh, 2, units, 2 * CAP, fe + LANES), BF),
            pltpu.VMEM((n_half, 2 * hr, fe), BF),
            pltpu.VMEM((n_half, 2 * hr, fe), BF),
            pltpu.VMEM((n_half, 2 * hr, 2 * hid), F32),
            pltpu.VMEM((2, n_half, hr, 3 * hid), BF),
            pltpu.VMEM((2, n_half, hr, 3 * hid), BF),
            pltpu.VMEM((2, n_half, 2 * hr + 16, hid), BF),
            pltpu.VMEM((nzh, 2, 2 * hr + 16, hid), BF),
            pltpu.VMEM((fe, hid), BF),
            pltpu.VMEM((all_rows, hid), BF),
            pltpu.VMEM((all_rows, hid), BF),
            pltpu.VMEM((nzh, units, 2 * CAP, fe // 2 + LANES), BF),
            pltpu.VMEM((nzh, units, 2 * CAP, fe // 2 + LANES), BF),
            pltpu.VMEM((nzh, WINDOW, 2 * CAP, fe // 2 + LANES), BF),
            pltpu.VMEM((nzh, WINDOW, 2 * CAP, fe // 2 + LANES), BF),
            pltpu.VMEM((WINDOW, 2 * CAP, fe // 2 + LANES), F32),
            dma((nzh + 2,)), dma((nzh + 2,)),
            dma((nzh,)), dma((nzh,)),
            dma((nzh,)), dma((nzh,)),
            dma((2,)), dma((2, n_half)),
            dma((2,)), dma((2, n_half)),
            dma((nzh, 2)), dma((nzh, 2)),
            dma((nzh,)), dma((nzh,)),
            dma((nzh,)), dma((nzh,)),
            dma, dma,
            dma((4,)),
        ],
        compiler_params=pltpu.CompilerParams(
            collective_id=0, has_side_effects=True, vmem_limit_bytes=58 * 1024 * 1024
        ),
    )(tokens, grad_out, routes.T, gates.T, w_in, w_out)
    return grad_tokens, grad_gates.T, grad_w_in, grad_w_out


def solution(mesh):
    dims = (X_CHIPS, ZH_CHIPS, mesh.shape["local"] // 2, mesh.shape["edata"])
    in_specs = (
        P(("node", "local"), "edata"),
        P(("node", "local"), "edata"),
        P(("node", "local"), None),
        P(("node", "local"), None),
        P("edata", ("node", "local")),
        P(("node", "local"), "edata"),
    )
    out_specs = (
        P(("node", "local"), "edata"),
        P(("node", "local"), None),
        P("edata", ("node", "local")),
        P(("node", "local"), "edata"),
    )
    return jax.shard_map(
        functools.partial(body, dims), mesh=mesh, in_specs=in_specs, out_specs=out_specs, check_vma=False
    )
```

```python
import functools

import jax
import jax.numpy as jnp
from jax import lax
from jax.experimental import pallas as pl
from jax.experimental.pallas import tpu as pltpu
from jax.sharding import PartitionSpec as P

MESH = pl.DeviceIdType.MESH
BF, F32 = jnp.bfloat16, jnp.float32
WINDOW = 2
CAP = 8
LANES = 128
X_CHIPS, ZH_CHIPS = 4, 4
HOP = 2
OWN_LAST = False


def half_chunks(nzh):
    if OWN_LAST:
        return [(0, 0)] + [(i, j) for i in range(1, nzh) for j in range(2)] + [(0, 1)]
    return [(i, j) for i in range(nzh) for j in range(2)]


def pick(table, t):
    value = table[0]
    for k in range(1, len(table)):
        value = jnp.where(t == k, table[k], value)
    return value


def gelu_pair(pre):
    coefficient = 0.7978845608028654
    tanh_val = jnp.tanh(coefficient * (pre + 0.044715 * pre * pre * pre))
    activation = 0.5 * pre * (1.0 + tanh_val)
    slopes = 0.5 * (1.0 + tanh_val) + 0.5 * pre * (1.0 - tanh_val * tanh_val) * coefficient * (
        1.0 + 3.0 * 0.044715 * pre * pre
    )
    return activation, slopes


def split(value):
    high = value.astype(BF)
    return high, (value - high.astype(F32)).astype(BF)


def dot_nt(a, b):
    return lax.dot_general(a, b, (((1,), (1,)), ((), ())), preferred_element_type=F32)


def dot_tn(a, b):
    return lax.dot_general(a, b, (((0,), (0,)), ((), ())), preferred_element_type=F32)


def wait_for(ref, sem):
    pltpu.make_async_copy(ref, ref, sem).wait()


def kernel(
    dims,
    tokens_hbm, grad_out_hbm, routes, gates, w_in_hbm, w_out_hbm,
    o_tokens, o_gates, o_w_in, o_w_out,
    tokens, grad_out, w_in, w_out, zbuf, rows, xa, dya, part, rs_out, rs_in, res, res_sib, w_sib, dpa, sca, cs, cr, zs, zr, own,
    z_s, z_r, xy_s, xy_r, sib_s, sib_r, rs_s, rs_r, ag_s, ag_r, ds_s, ds_r, c_s, c_r, zc_s, zc_r, w_s, w_r, in_sem,
):
    nx, nzh, ny, nzl = dims
    units = nx * ny
    half = units // 2
    hr = half * CAP
    n_half = 2 * nzh
    tok, fe = tokens.shape
    hid = w_in.shape[1]
    fh = fe // 2
    lat = 2 * HOP * (nzl - 1)
    offsets = list(range(nzh))
    near = [1, 3] if nzh == 4 else list(range(1, nzh))
    far = 2 if nzh == 4 else None

    node, local, zl = lax.axis_index("node"), lax.axis_index("local"), lax.axis_index("edata")
    x, zh, y, c = node // nzh, node % nzh, local // 2, local % 2
    me = y * nx + x
    sibling = (node, y * 2 + 1 - c, zl)

    def at_unit(u):
        return ((u % nx) * nzh + zh, (u // nx) * 2 + c, zl)

    def at_zh(other):
        return (x * nzh + other, local, zl)

    order = half_chunks(nzh)
    ends = {i: order.index((i, 1)) for i in range(nzh)}

    def chunk_of(t):
        return pick([i for i, _ in order], t)

    def which_of(t):
        return pick([j for _, j in order], t)

    pos = (nzl - 1 - zl, zl)
    ahead = (zl - 1, zl + 1)
    behind = (zl + 1, zl - 1)

    def remote(src, dst, send_sem, recv_sem, device):
        return pltpu.make_async_remote_copy(
            src_ref=src, dst_ref=dst, send_sem=send_sem, recv_sem=recv_sem, device_id=device, device_id_type=MESH
        )

    loads = [
        pltpu.make_async_copy(src, dst, in_sem.at[n])
        for n, (src, dst) in enumerate(
            ((tokens_hbm, tokens), (grad_out_hbm, grad_out), (w_in_hbm, w_in), (w_out_hbm, w_out))
        )
    ]
    for load in loads:
        load.start()

    barrier = pltpu.get_barrier_semaphore()

    def greet(device):
        pl.semaphore_signal(barrier, inc=1, device_id=device, device_id_type=MESH)

    greet(sibling)
    for o in range(1, nzh):
        greet(at_zh((zh + o) % nzh))

    @pl.loop(1, units)
    def _(d):
        greet(at_unit((me + d) % units))

    @pl.when(zl > 0)
    def _():
        greet((node, local, zl - 1))

    @pl.when(zl < nzl - 1)
    def _():
        greet((node, local, zl + 1))

    slot_rows = 3 * WINDOW * CAP
    row = lax.broadcasted_iota(jnp.int32, (slot_rows, tok), 0)
    expert_of, place_of = (row // CAP) % WINDOW, row % CAP
    r0, r1 = routes[0:1, :], routes[1:2, :]
    g0, g1 = gates[0:1, :].astype(F32), gates[1:2, :].astype(F32)
    named = (r0 == expert_of) | (r1 == expert_of)
    earlier = lax.broadcasted_iota(jnp.int32, (tok, tok), 0) < lax.broadcasted_iota(jnp.int32, (tok, tok), 1)
    position = jnp.dot(
        jnp.where(named, 1.0, 0.0).astype(BF), jnp.where(earlier, 1.0, 0.0).astype(BF), preferred_element_type=F32
    )
    hot_f = jnp.where(named & (position == place_of.astype(F32)), 1.0, 0.0)
    hot = hot_f.astype(BF)
    send_g = jnp.sum(hot_f * jnp.where(r0 == expert_of, g0, g1), axis=1, keepdims=True)
    send_g = jnp.broadcast_to(send_g, (slot_rows, LANES))
    loads[0].wait()
    send_x = jnp.dot(hot, tokens[...], preferred_element_type=F32)
    loads[1].wait()
    send_dy = jnp.dot(hot, grad_out[...], preferred_element_type=F32)
    for e in range(WINDOW):
        mine = slice(e * CAP, (e + 1) * CAP)
        zbuf[0, e, :, :fe] = jnp.concatenate([send_x[mine], send_dy[mine]], axis=0).astype(BF)
        zbuf[0, e, :, fe:] = jnp.concatenate([send_g[mine], send_g[mine]], axis=0).astype(BF)

    greeted = 1 + (nzh - 1) + (units - 1) + jnp.where(zl > 0, 1, 0) + jnp.where(zl < nzl - 1, 1, 0)
    pl.semaphore_wait(barrier, greeted)

    def dispatch(i, e):
        @pl.loop(0, units // 2)
        def _(d):
            xx = e * (nx // 2) + (x + d) % (nx // 2)
            yy = (y + d // (nx // 2)) % ny
            src, dst = zbuf.at[i, e], rows.at[i, c, me]
            itself = (d == 0) & (x // (nx // 2) == e)

            @pl.when(jnp.logical_not(itself))
            def _():
                remote(src, dst, xy_s.at[i], xy_r.at[i], at_unit(yy * nx + xx)).start()

            @pl.when(itself)
            def _():
                pltpu.make_async_copy(src, dst, xy_r.at[i]).start()

    for i in near:
        for e in range(WINDOW):
            remote(
                zbuf.at[0, e], zbuf.at[i, e], z_s.at[i, e], z_r.at[i, e], at_zh((zh + nzh - offsets[i]) % nzh)
            ).start()
    for e in range(WINDOW):
        dispatch(0, e)
    loads[2].wait()
    remote(w_in, w_sib, w_s, w_r, sibling).start()
    loads[3].wait()

    def hand_on(i, e):
        @pl.when(jnp.logical_not((i == near[-1]) & (e == len(near) - 1) & (far is not None)))
        def _():
            wait_for(zbuf.at[i, e], z_r.at[i, e])

        dispatch(i, e)

    def relay():
        if far is not None:
            for e, k in enumerate(near):
                if k != 1:
                    wait_for(zbuf.at[k, e], z_r.at[k, e])
                remote(
                    zbuf.at[k, e], zbuf.at[far, e], z_s.at[far, e], z_r.at[far, e], at_zh((zh + nzh - k) % nzh)
                ).start()

    def pass_on(h, t, pre, back):
        high, low = split(pre)
        rs_out[h, t, :, 0:hid] = high
        rs_out[h, t, :, hid : 2 * hid] = low
        rs_out[h, t, :, 2 * hid :] = back.astype(BF)
        remote(
            rs_out.at[h, t], rs_in.at[h, t], rs_s.at[h], rs_r.at[h, t], (node, local, ahead[h])
        ).start()

    def send_back(h, t):
        remote(
            res.at[h, t], res.at[h, t], ag_s.at[h], ag_r.at[h, t], (node, local, behind[h])
        ).start()

    def partial_products(t):
        i, j = chunk_of(t), which_of(t)
        parity = (c + j) % 2

        @pl.when(j == 0)
        def _():
            wait_for(rows.at[i, c], xy_r.at[i])
            remote(rows.at[i, c], rows.at[i, c], sib_s.at[i], sib_r.at[i], sibling).start()

        @pl.when(j == 1)
        def _():
            wait_for(rows.at[i, 1 - c], sib_r.at[i])

        for q in range(half):
            a = rows[i, parity, 2 * q, :, :fe].astype(F32)
            b = rows[i, parity, 2 * q + 1, :, :fe].astype(F32)
            xa[t, q * 16 : (q + 1) * 16, :] = jnp.concatenate([a[:CAP], b[:CAP]], axis=0).astype(BF)
            dya[t, q * 16 : (q + 1) * 16, :] = jnp.concatenate([a[CAP:], b[CAP:]], axis=0).astype(BF)
        part[t, :, :hid] = jnp.dot(xa[t], w_in[...], preferred_element_type=F32)
        part[t, :, hid:] = dot_nt(dya[t], w_out[...])
        for h in range(2):

            @pl.when(pos[h] == 0)
            def _():
                mine = slice(h * hr, (h + 1) * hr)
                pass_on(h, t, part[t, mine, :hid], part[t, mine, hid:])

    def sum_step(h, t):
        wait_for(rs_in.at[h, t], rs_r.at[h, t])
        mine = slice(h * hr, (h + 1) * hr)
        came = rs_in[h, t].astype(F32)
        pre = (came[:, :hid] + came[:, hid : 2 * hid]) + part[t, mine, :hid]
        back = came[:, 2 * hid :] + part[t, mine, hid:]

        @pl.when(pos[h] < nzl - 1)
        def _():
            pass_on(h, t, pre, back)

        @pl.when(pos[h] == nzl - 1)
        def _():
            i, parity = chunk_of(t), (c + which_of(t)) % 2
            gate = rows[i, parity, h * half : (h + 1) * half, :, fe:].astype(F32)[:, :CAP]
            gate = gate.reshape(hr, LANES)
            gate = jnp.concatenate([gate] * (hid // LANES), axis=1)
            activation, slopes = gelu_pair(pre)
            res[h, t, :hr, :] = (gate * back * slopes).astype(BF)
            res[h, t, hr : 2 * hr, :] = (gate * activation).astype(BF)
            sums = jnp.sum(activation * back, axis=1, keepdims=True)
            small_lane = lax.broadcasted_iota(jnp.int32, (CAP, LANES), 1)
            packed = jnp.zeros((CAP, LANES), F32)
            for u in range(half):
                packed = jnp.where(small_lane == h * half + u, sums[u * CAP : (u + 1) * CAP], packed)
            high = packed.astype(BF).astype(F32)
            both = jnp.concatenate([high, packed - high], axis=0)
            both = jnp.concatenate([both] * (hid // LANES), axis=1)
            res[h, t, 2 * hr :, :] = both.astype(BF)
            send_back(h, t)

    def back_step(h, t):
        wait_for(res.at[h, t], ag_r.at[h, t])

        @pl.when(pos[h] > 0)
        def _():
            send_back(h, t)

    def keep(t):
        for h in range(2):
            mine = pl.ds(pl.multiple_of(t * 2 * hr + h * hr, hr), hr)
            dpa[mine, :] = res[h, t, :hr, :]
            sca[mine, :] = res[h, t, hr : 2 * hr, :]

    def to_sibling(i):
        for h in range(2):
            remote(res.at[h, pick([ends[k] for k in range(nzh)], i)], res_sib.at[i, h], ds_s.at[i, h], ds_r.at[i, h], sibling).start()

    def combine(i):
        t = pick([order.index((k, 0)) for k in range(nzh)], i)
        for h in range(2):
            wait_for(res_sib.at[i, h], ds_r.at[i, h])

        d_own = jnp.concatenate([res[0, t, :hr, :], res[1, t, :hr, :]], axis=0)
        d_sib = jnp.concatenate([res_sib[i, 0, :hr, :], res_sib[i, 1, :hr, :]], axis=0)
        total = dot_nt(d_own, w_in[...]) + dot_nt(d_sib, w_sib[...])
        packed = jnp.zeros((CAP, LANES), F32)
        for h in range(2):
            for ref in (res[h, t, 2 * hr :, :LANES], res_sib[i, h, 2 * hr :, :LANES]):
                both = ref.astype(F32)
                packed = packed + (both[:CAP] + both[CAP:])
        high = packed.astype(BF).astype(F32)
        gates_of_all = jnp.concatenate([high, packed - high], axis=0).astype(BF)
        for u in range(units):
            mine = total[u * CAP : (u + 1) * CAP]
            cs[i, u, :, :fh] = jnp.concatenate([mine[:, :fh], mine[:, fh:]], axis=0).astype(BF)
            cs[i, u, :, fh:] = gates_of_all

    def send_units(i, first, last):
        @pl.loop(first, last)
        def _(d):
            u = (me + d) % units

            @pl.when(d > 0)
            def _():
                remote(cs.at[i, u], cr.at[i, me], c_s.at[i], c_r.at[i], at_unit(u)).start()

            @pl.when(d == 0)
            def _():
                pltpu.make_async_copy(cs.at[i, u], cr.at[i, me], c_r.at[i]).start()

    def sum_units(i):
        wait_for(cr.at[i], c_r.at[i])
        for e in range(WINDOW):
            total = jnp.zeros((2 * CAP, fh + LANES), F32)
            for yy in range(ny):
                for xx in range(e * (nx // 2), (e + 1) * (nx // 2)):
                    total = total + cr[i, yy * nx + xx].astype(F32)

            @pl.when(i == 0)
            def _():
                own[e] = total

            @pl.when(i > 0)
            def _():
                gate = total[:CAP, fh:] + total[CAP:, fh:]
                high = gate.astype(BF).astype(F32)
                zs[i, e, :, :fh] = total[:, :fh].astype(BF)
                zs[i, e, :, fh:] = jnp.concatenate([high, gate - high], axis=0).astype(BF)

        @pl.when(i > 0)
        def _():
            remote(
                zs.at[i], zr.at[i], zc_s.at[i], zc_r.at[i], at_zh((zh + pick(offsets, i)) % nzh)
            ).start()

    tile = min(256, fe)

    @pl.loop(0, n_half + lat)
    def _(s):
        if nzh > 1:

            @pl.when(s == 0)
            def _():
                hand_on(1, 0)
                hand_on(1, 1)
                relay()

        @pl.when((s > 0) & (s < 2 * nzh - 3))
        def _():
            hand_on((s + 3) // 2, (s + 1) % 2)

        @pl.when(s < n_half)
        def _():
            partial_products(s)

        for h in range(2):
            t = s - HOP * pos[h]

            @pl.when((pos[h] > 0) & (t >= 0) & (t < n_half))
            def _():
                sum_step(h, t)

        for h in range(2):
            t = s - lat + HOP * pos[h]

            @pl.when((pos[h] < nzl - 1) & (t >= 0) & (t < n_half))
            def _():
                back_step(h, t)

        done = s - lat

        @pl.when(done >= 0)
        def _():
            @pl.when(done == 0)
            def _():
                wait_for(w_sib, w_r)

            keep(done)

            @pl.when(which_of(done) == 1)
            def _():
                to_sibling(chunk_of(done))

        @pl.when((done >= 1) & (which_of(done - 1) == 1))
        def _():
            combine(chunk_of(done - 1))
            send_units(chunk_of(done - 1), 0, units // 2)

        @pl.when((done >= 2) & (which_of(done - 2) == 1))
        def _():
            send_units(chunk_of(done - 2), units // 2, units)

        @pl.when((done >= 4) & (which_of(done - 4) == 1))
        def _():
            sum_units(chunk_of(done - 4))

    def finish_w_out(first, last):
        @pl.loop(first, last)
        def _(m):
            cols = pl.ds(pl.multiple_of(m * tile, tile), tile)
            o_w_out[:, cols] = dot_tn(sca[...], dya[:, :, cols].reshape(n_half * 2 * hr, tile))

    tiles = fe // tile
    finish_w_out(0, tiles // 2)
    for t, (i, j) in enumerate(order):
        if j == 1 and t == n_half - 2:
            send_units(i, units // 2, units)
    combine(order[-1][0])
    send_units(order[-1][0], 0, units)
    late = [i for t, (i, j) in enumerate(order) if j == 1 and t >= n_half - 4]
    for i in late[:-1]:
        sum_units(i)
    finish_w_out(tiles // 2, tiles)
    sum_units(late[-1])

    @pl.loop(0, tiles)
    def _(m):
        cols = pl.ds(pl.multiple_of(m * tile, tile), tile)
        o_w_in[cols, :] = dot_tn(xa[:, :, cols].reshape(n_half * 2 * hr, tile), dpa[...])

    slot, gate_slot = [], []
    for i in range(1, nzh):
        wait_for(zr.at[i], zc_r.at[i])
    for e in range(WINDOW):
        total = own[e]
        for i in range(1, nzh):
            total = total + zr[i, e].astype(F32)
        slot.append(jnp.concatenate([total[:CAP, :fh], total[CAP:, :fh]], axis=1))
        gate = jnp.where(
            lax.broadcasted_iota(jnp.int32, (CAP, LANES), 1) == me, total[:CAP, fh:] + total[CAP:, fh:], 0.0
        )
        gate_slot.append(jnp.broadcast_to(jnp.sum(gate, axis=1, keepdims=True), (CAP, LANES)))
    slot = jnp.concatenate(slot, axis=0)
    high = slot.astype(BF).astype(F32)
    middle = (slot - high).astype(BF).astype(F32)
    o_tokens[...] = dot_tn(hot, jnp.concatenate([high, middle, slot - high - middle], axis=0).astype(BF)).astype(BF)
    gate_slot = jnp.concatenate(gate_slot, axis=0)
    gate_slot = jnp.concatenate([gate_slot] * (tok // LANES), axis=1) * hot_f[: WINDOW * CAP]
    for k, r in enumerate((r0, r1)):
        kept = jnp.where(r == expert_of[: WINDOW * CAP], gate_slot, 0.0)
        o_gates[k : k + 1, :] = jnp.sum(kept, axis=0, keepdims=True)

    for i in range(1, nzh):
        wait_for(zs.at[i], zc_s.at[i])
    for i in range(1, nzh):
        for e in range(WINDOW):
            wait_for(zbuf.at[i, e], z_s.at[i, e])
    for i in range(nzh):
        wait_for(rows.at[i, 0, pl.ds(0, units - 1)], xy_s.at[i])
        wait_for(rows.at[i, 0], sib_s.at[i])
        wait_for(cs.at[i, pl.ds(0, units - 1)], c_s.at[i])
        for h in range(2):
            wait_for(res_sib.at[i, h], ds_s.at[i, h])
    wait_for(w_sib, w_s)
    for h in range(2):

        @pl.when(pos[h] < nzl - 1)
        def _():
            wait_for(rs_out.at[h], rs_s.at[h])

        @pl.when(pos[h] > 0)
        def _():
            wait_for(res.at[h], ag_s.at[h])


def body(dims, tokens, grad_out, routes, gates, w_in, w_out):
    nx, nzh, ny, nzl = dims
    units = nx * ny
    hr = units * CAP // 2
    n_half = 2 * nzh
    tok, fe = tokens.shape
    hid = w_in.shape[1]
    all_rows = n_half * 2 * hr
    vmem, hbm = pl.BlockSpec(memory_space=pltpu.VMEM), pl.BlockSpec(memory_space=pltpu.HBM)
    dma = pltpu.SemaphoreType.DMA
    grad_tokens, grad_gates, grad_w_in, grad_w_out = pl.pallas_call(
        functools.partial(kernel, dims),
        out_shape=(
            pltpu.VMEM((tok, fe), BF),
            pltpu.VMEM((2, tok), F32),
            pltpu.VMEM((fe, hid), F32),
            pltpu.VMEM((hid, fe), F32),
        ),
        in_specs=[hbm, hbm, vmem, vmem, hbm, hbm],
        out_specs=(vmem,) * 4,
        scratch_shapes=[
            pltpu.VMEM((tok, fe), BF),
            pltpu.VMEM((tok, fe), BF),
            pltpu.VMEM((fe, hid), BF),
            pltpu.VMEM((hid, fe), BF),
            pltpu.VMEM((nzh, WINDOW, 2 * CAP, fe + LANES), BF),
            pltpu.VMEM((nzh, 2, units, 2 * CAP, fe + LANES), BF),
            pltpu.VMEM((n_half, 2 * hr, fe), BF),
            pltpu.VMEM((n_half, 2 * hr, fe), BF),
            pltpu.VMEM((n_half, 2 * hr, 2 * hid), F32),
            pltpu.VMEM((2, n_half, hr, 3 * hid), BF),
            pltpu.VMEM((2, n_half, hr, 3 * hid), BF),
            pltpu.VMEM((2, n_half, 2 * hr + 16, hid), BF),
            pltpu.VMEM((nzh, 2, 2 * hr + 16, hid), BF),
            pltpu.VMEM((fe, hid), BF),
            pltpu.VMEM((all_rows, hid), BF),
            pltpu.VMEM((all_rows, hid), BF),
            pltpu.VMEM((nzh, units, 2 * CAP, fe // 2 + LANES), BF),
            pltpu.VMEM((nzh, units, 2 * CAP, fe // 2 + LANES), BF),
            pltpu.VMEM((nzh, WINDOW, 2 * CAP, fe // 2 + LANES), BF),
            pltpu.VMEM((nzh, WINDOW, 2 * CAP, fe // 2 + LANES), BF),
            pltpu.VMEM((WINDOW, 2 * CAP, fe // 2 + LANES), F32),
            dma((nzh, WINDOW)), dma((nzh, WINDOW)),
            dma((nzh,)), dma((nzh,)),
            dma((nzh,)), dma((nzh,)),
            dma((2,)), dma((2, n_half)),
            dma((2,)), dma((2, n_half)),
            dma((nzh, 2)), dma((nzh, 2)),
            dma((nzh,)), dma((nzh,)),
            dma((nzh,)), dma((nzh,)),
            dma, dma,
            dma((4,)),
        ],
        compiler_params=pltpu.CompilerParams(
            collective_id=0, has_side_effects=True, vmem_limit_bytes=58 * 1024 * 1024
        ),
    )(tokens, grad_out, routes.T, gates.T, w_in, w_out)
    return grad_tokens, grad_gates.T, grad_w_in, grad_w_out


def solution(mesh):
    dims = (X_CHIPS, ZH_CHIPS, mesh.shape["local"] // 2, mesh.shape["edata"])
    in_specs = (
        P(("node", "local"), "edata"),
        P(("node", "local"), "edata"),
        P(("node", "local"), None),
        P(("node", "local"), None),
        P("edata", ("node", "local")),
        P(("node", "local"), "edata"),
    )
    out_specs = (
        P(("node", "local"), "edata"),
        P(("node", "local"), None),
        P("edata", ("node", "local")),
        P(("node", "local"), "edata"),
    )
    return jax.shard_map(
        functools.partial(body, dims), mesh=mesh, in_specs=in_specs, out_specs=out_specs, check_vma=False
    )
```

```python
import functools

import jax
import jax.numpy as jnp
from jax import lax
from jax.experimental import pallas as pl
from jax.experimental.pallas import tpu as pltpu
from jax.sharding import PartitionSpec as P

MESH = pl.DeviceIdType.MESH
BF, F32 = jnp.bfloat16, jnp.float32
WINDOW = 2
CAP = 8
LANES = 128
X_CHIPS, ZH_CHIPS = 4, 4
HOP = 1
OWN_LAST = False


def half_chunks(nzh):
    if OWN_LAST:
        return [(0, 0)] + [(i, j) for i in range(1, nzh) for j in range(2)] + [(0, 1)]
    return [(i, j) for i in range(nzh) for j in range(2)]


def pick(table, t):
    value = table[0]
    for k in range(1, len(table)):
        value = jnp.where(t == k, table[k], value)
    return value


def gelu_pair(pre):
    coefficient = 0.7978845608028654
    tanh_val = jnp.tanh(coefficient * (pre + 0.044715 * pre * pre * pre))
    activation = 0.5 * pre * (1.0 + tanh_val)
    slopes = 0.5 * (1.0 + tanh_val) + 0.5 * pre * (1.0 - tanh_val * tanh_val) * coefficient * (
        1.0 + 3.0 * 0.044715 * pre * pre
    )
    return activation, slopes


def split(value):
    high = value.astype(BF)
    return high, (value - high.astype(F32)).astype(BF)


def dot_nt(a, b):
    return lax.dot_general(a, b, (((1,), (1,)), ((), ())), preferred_element_type=F32)


def dot_tn(a, b):
    return lax.dot_general(a, b, (((0,), (0,)), ((), ())), preferred_element_type=F32)


def wait_for(ref, sem):
    pltpu.make_async_copy(ref, ref, sem).wait()


def kernel(
    dims,
    tokens_hbm, grad_out_hbm, routes, gates, w_in_hbm, w_out_hbm,
    o_tokens, o_gates, o_w_in, o_w_out,
    tokens, grad_out, w_in, w_out, zbuf, rows, xa, dya, part, rs_out, rs_in, res, res_sib, w_sib, dpa, sca, cs, cr, zs, zr, own,
    z_s, z_r, xy_s, xy_r, sib_s, sib_r, rs_s, rs_r, ag_s, ag_r, ds_s, ds_r, c_s, c_r, zc_s, zc_r, w_s, w_r, in_sem,
):
    nx, nzh, ny, nzl = dims
    units = nx * ny
    half = units // 2
    hr = half * CAP
    n_half = 2 * nzh
    tok, fe = tokens.shape
    hid = w_in.shape[1]
    fh = fe // 2
    lat = 2 * HOP * (nzl - 1)
    offsets = list(range(nzh))
    near = [1, 3] if nzh == 4 else list(range(1, nzh))
    far = 2 if nzh == 4 else None

    node, local, zl = lax.axis_index("node"), lax.axis_index("local"), lax.axis_index("edata")
    x, zh, y, c = node // nzh, node % nzh, local // 2, local % 2
    me = y * nx + x
    sibling = (node, y * 2 + 1 - c, zl)

    def at_unit(u):
        return ((u % nx) * nzh + zh, (u // nx) * 2 + c, zl)

    def at_zh(other):
        return (x * nzh + other, local, zl)

    order = half_chunks(nzh)
    ends = {i: order.index((i, 1)) for i in range(nzh)}

    def chunk_of(t):
        return pick([i for i, _ in order], t)

    def which_of(t):
        return pick([j for _, j in order], t)

    pos = (nzl - 1 - zl, zl)
    ahead = (zl - 1, zl + 1)
    behind = (zl + 1, zl - 1)

    def remote(src, dst, send_sem, recv_sem, device):
        return pltpu.make_async_remote_copy(
            src_ref=src, dst_ref=dst, send_sem=send_sem, recv_sem=recv_sem, device_id=device, device_id_type=MESH
        )

    loads = [
        pltpu.make_async_copy(src, dst, in_sem.at[n])
        for n, (src, dst) in enumerate(
            ((tokens_hbm, tokens), (grad_out_hbm, grad_out), (w_in_hbm, w_in), (w_out_hbm, w_out))
        )
    ]
    for load in loads:
        load.start()

    barrier = pltpu.get_barrier_semaphore()

    def greet(device):
        pl.semaphore_signal(barrier, inc=1, device_id=device, device_id_type=MESH)

    greet(sibling)
    for o in range(1, nzh):
        greet(at_zh((zh + o) % nzh))

    @pl.loop(1, units)
    def _(d):
        greet(at_unit((me + d) % units))

    @pl.when(zl > 0)
    def _():
        greet((node, local, zl - 1))

    @pl.when(zl < nzl - 1)
    def _():
        greet((node, local, zl + 1))

    slot_rows = 3 * WINDOW * CAP
    row = lax.broadcasted_iota(jnp.int32, (slot_rows, tok), 0)
    expert_of, place_of = (row // CAP) % WINDOW, row % CAP
    r0, r1 = routes[0:1, :], routes[1:2, :]
    g0, g1 = gates[0:1, :].astype(F32), gates[1:2, :].astype(F32)
    named = (r0 == expert_of) | (r1 == expert_of)
    earlier = lax.broadcasted_iota(jnp.int32, (tok, tok), 0) < lax.broadcasted_iota(jnp.int32, (tok, tok), 1)
    position = jnp.dot(
        jnp.where(named, 1.0, 0.0).astype(BF), jnp.where(earlier, 1.0, 0.0).astype(BF), preferred_element_type=F32
    )
    hot_f = jnp.where(named & (position == place_of.astype(F32)), 1.0, 0.0)
    hot = hot_f.astype(BF)
    send_g = jnp.sum(hot_f * jnp.where(r0 == expert_of, g0, g1), axis=1, keepdims=True)
    send_g = jnp.broadcast_to(send_g, (slot_rows, LANES))
    loads[0].wait()
    send_x = jnp.dot(hot, tokens[...], preferred_element_type=F32)
    loads[1].wait()
    send_dy = jnp.dot(hot, grad_out[...], preferred_element_type=F32)
    for e in range(WINDOW):
        mine = slice(e * CAP, (e + 1) * CAP)
        zbuf[0, e, :, :fe] = jnp.concatenate([send_x[mine], send_dy[mine]], axis=0).astype(BF)
        zbuf[0, e, :, fe:] = jnp.concatenate([send_g[mine], send_g[mine]], axis=0).astype(BF)

    greeted = 1 + (nzh - 1) + (units - 1) + jnp.where(zl > 0, 1, 0) + jnp.where(zl < nzl - 1, 1, 0)
    pl.semaphore_wait(barrier, greeted)

    def dispatch(i, e):
        @pl.loop(0, units // 2)
        def _(d):
            xx = e * (nx // 2) + (x + d) % (nx // 2)
            yy = (y + d // (nx // 2)) % ny
            src, dst = zbuf.at[i, e], rows.at[i, c, me]
            itself = (d == 0) & (x // (nx // 2) == e)

            @pl.when(jnp.logical_not(itself))
            def _():
                remote(src, dst, xy_s.at[i], xy_r.at[i], at_unit(yy * nx + xx)).start()

            @pl.when(itself)
            def _():
                pltpu.make_async_copy(src, dst, xy_r.at[i]).start()

    for i in near:
        for e in range(WINDOW):
            remote(
                zbuf.at[0, e], zbuf.at[i, e], z_s.at[i, e], z_r.at[i, e], at_zh((zh + nzh - offsets[i]) % nzh)
            ).start()
    for e in range(WINDOW):
        dispatch(0, e)
    loads[2].wait()
    remote(w_in, w_sib, w_s, w_r, sibling).start()
    loads[3].wait()

    def hand_on(i, e):
        @pl.when(jnp.logical_not((i == near[-1]) & (e == len(near) - 1) & (far is not None)))
        def _():
            wait_for(zbuf.at[i, e], z_r.at[i, e])

        dispatch(i, e)

    def relay():
        if far is not None:
            for e, k in enumerate(near):
                if k != 1:
                    wait_for(zbuf.at[k, e], z_r.at[k, e])
                remote(
                    zbuf.at[k, e], zbuf.at[far, e], z_s.at[far, e], z_r.at[far, e], at_zh((zh + nzh - k) % nzh)
                ).start()

    def pass_on(h, t, pre, back):
        high, low = split(pre)
        rs_out[h, t, :, 0:hid] = high
        rs_out[h, t, :, hid : 2 * hid] = low
        rs_out[h, t, :, 2 * hid :] = back.astype(BF)
        remote(
            rs_out.at[h, t], rs_in.at[h, t], rs_s.at[h], rs_r.at[h, t], (node, local, ahead[h])
        ).start()

    def send_back(h, t):
        remote(
            res.at[h, t], res.at[h, t], ag_s.at[h], ag_r.at[h, t], (node, local, behind[h])
        ).start()

    def partial_products(t):
        i, j = chunk_of(t), which_of(t)
        parity = (c + j) % 2

        @pl.when(j == 0)
        def _():
            wait_for(rows.at[i, c], xy_r.at[i])
            remote(rows.at[i, c], rows.at[i, c], sib_s.at[i], sib_r.at[i], sibling).start()

        @pl.when(j == 1)
        def _():
            wait_for(rows.at[i, 1 - c], sib_r.at[i])

        for q in range(half):
            a = rows[i, parity, 2 * q, :, :fe].astype(F32)
            b = rows[i, parity, 2 * q + 1, :, :fe].astype(F32)
            xa[t, q * 16 : (q + 1) * 16, :] = jnp.concatenate([a[:CAP], b[:CAP]], axis=0).astype(BF)
            dya[t, q * 16 : (q + 1) * 16, :] = jnp.concatenate([a[CAP:], b[CAP:]], axis=0).astype(BF)
        part[t, :, :hid] = jnp.dot(xa[t], w_in[...], preferred_element_type=F32)
        part[t, :, hid:] = dot_nt(dya[t], w_out[...])
        for h in range(2):

            @pl.when(pos[h] == 0)
            def _():
                mine = slice(h * hr, (h + 1) * hr)
                pass_on(h, t, part[t, mine, :hid], part[t, mine, hid:])

    def sum_step(h, t):
        wait_for(rs_in.at[h, t], rs_r.at[h, t])
        mine = slice(h * hr, (h + 1) * hr)
        came = rs_in[h, t].astype(F32)
        pre = (came[:, :hid] + came[:, hid : 2 * hid]) + part[t, mine, :hid]
        back = came[:, 2 * hid :] + part[t, mine, hid:]

        @pl.when(pos[h] < nzl - 1)
        def _():
            pass_on(h, t, pre, back)

        @pl.when(pos[h] == nzl - 1)
        def _():
            i, parity = chunk_of(t), (c + which_of(t)) % 2
            gate = rows[i, parity, h * half : (h + 1) * half, :, fe:].astype(F32)[:, :CAP]
            gate = gate.reshape(hr, LANES)
            gate = jnp.concatenate([gate] * (hid // LANES), axis=1)
            activation, slopes = gelu_pair(pre)
            res[h, t, :hr, :] = (gate * back * slopes).astype(BF)
            res[h, t, hr : 2 * hr, :] = (gate * activation).astype(BF)
            sums = jnp.sum(activation * back, axis=1, keepdims=True)
            small_lane = lax.broadcasted_iota(jnp.int32, (CAP, LANES), 1)
            packed = jnp.zeros((CAP, LANES), F32)
            for u in range(half):
                packed = jnp.where(small_lane == h * half + u, sums[u * CAP : (u + 1) * CAP], packed)
            high = packed.astype(BF).astype(F32)
            both = jnp.concatenate([high, packed - high], axis=0)
            both = jnp.concatenate([both] * (hid // LANES), axis=1)
            res[h, t, 2 * hr :, :] = both.astype(BF)
            send_back(h, t)

    def back_step(h, t):
        wait_for(res.at[h, t], ag_r.at[h, t])

        @pl.when(pos[h] > 0)
        def _():
            send_back(h, t)

    def keep(t):
        for h in range(2):
            mine = pl.ds(pl.multiple_of(t * 2 * hr + h * hr, hr), hr)
            dpa[mine, :] = res[h, t, :hr, :]
            sca[mine, :] = res[h, t, hr : 2 * hr, :]

    def to_sibling(i):
        for h in range(2):
            remote(res.at[h, pick([ends[k] for k in range(nzh)], i)], res_sib.at[i, h], ds_s.at[i, h], ds_r.at[i, h], sibling).start()

    def combine(i):
        t = pick([order.index((k, 0)) for k in range(nzh)], i)
        for h in range(2):
            wait_for(res_sib.at[i, h], ds_r.at[i, h])

        d_own = jnp.concatenate([res[0, t, :hr, :], res[1, t, :hr, :]], axis=0)
        d_sib = jnp.concatenate([res_sib[i, 0, :hr, :], res_sib[i, 1, :hr, :]], axis=0)
        total = dot_nt(d_own, w_in[...]) + dot_nt(d_sib, w_sib[...])
        packed = jnp.zeros((CAP, LANES), F32)
        for h in range(2):
            for ref in (res[h, t, 2 * hr :, :LANES], res_sib[i, h, 2 * hr :, :LANES]):
                both = ref.astype(F32)
                packed = packed + (both[:CAP] + both[CAP:])
        high = packed.astype(BF).astype(F32)
        gates_of_all = jnp.concatenate([high, packed - high], axis=0).astype(BF)
        for u in range(units):
            mine = total[u * CAP : (u + 1) * CAP]
            cs[i, u, :, :fh] = jnp.concatenate([mine[:, :fh], mine[:, fh:]], axis=0).astype(BF)
            cs[i, u, :, fh:] = gates_of_all

    def send_units(i, first, last):
        @pl.loop(first, last)
        def _(d):
            u = (me + d) % units

            @pl.when(d > 0)
            def _():
                remote(cs.at[i, u], cr.at[i, me], c_s.at[i], c_r.at[i], at_unit(u)).start()

            @pl.when(d == 0)
            def _():
                pltpu.make_async_copy(cs.at[i, u], cr.at[i, me], c_r.at[i]).start()

    def sum_units(i):
        wait_for(cr.at[i], c_r.at[i])
        for e in range(WINDOW):
            total = jnp.zeros((2 * CAP, fh + LANES), F32)
            for yy in range(ny):
                for xx in range(e * (nx // 2), (e + 1) * (nx // 2)):
                    total = total + cr[i, yy * nx + xx].astype(F32)

            @pl.when(i == 0)
            def _():
                own[e] = total

            @pl.when(i > 0)
            def _():
                gate = total[:CAP, fh:] + total[CAP:, fh:]
                high = gate.astype(BF).astype(F32)
                zs[i, e, :, :fh] = total[:, :fh].astype(BF)
                zs[i, e, :, fh:] = jnp.concatenate([high, gate - high], axis=0).astype(BF)

        @pl.when(i > 0)
        def _():
            remote(
                zs.at[i], zr.at[i], zc_s.at[i], zc_r.at[i], at_zh((zh + pick(offsets, i)) % nzh)
            ).start()

    tile = min(256, fe)

    @pl.loop(0, n_half + lat)
    def _(s):
        if nzh > 1:

            @pl.when(s == 0)
            def _():
                hand_on(1, 0)
                hand_on(1, 1)
                relay()

        @pl.when((s > 0) & (s < 2 * nzh - 3))
        def _():
            hand_on((s + 3) // 2, (s + 1) % 2)

        @pl.when(s < n_half)
        def _():
            partial_products(s)

        for h in range(2):
            t = s - HOP * pos[h]

            @pl.when((pos[h] > 0) & (t >= 0) & (t < n_half))
            def _():
                sum_step(h, t)

        for h in range(2):
            t = s - lat + HOP * pos[h]

            @pl.when((pos[h] < nzl - 1) & (t >= 0) & (t < n_half))
            def _():
                back_step(h, t)

        done = s - lat

        @pl.when(done >= 0)
        def _():
            @pl.when(done == 0)
            def _():
                wait_for(w_sib, w_r)

            keep(done)

            @pl.when(which_of(done) == 1)
            def _():
                to_sibling(chunk_of(done))

        @pl.when((done >= 1) & (which_of(done - 1) == 1))
        def _():
            combine(chunk_of(done - 1))
            send_units(chunk_of(done - 1), 0, units // 2)

        @pl.when((done >= 2) & (which_of(done - 2) == 1))
        def _():
            send_units(chunk_of(done - 2), units // 2, units)

        @pl.when((done >= 4) & (which_of(done - 4) == 1))
        def _():
            sum_units(chunk_of(done - 4))

    def finish_w_out(first, last):
        @pl.loop(first, last)
        def _(m):
            cols = pl.ds(pl.multiple_of(m * tile, tile), tile)
            o_w_out[:, cols] = dot_tn(sca[...], dya[:, :, cols].reshape(n_half * 2 * hr, tile))

    tiles = fe // tile
    finish_w_out(0, tiles // 2)
    for t, (i, j) in enumerate(order):
        if j == 1 and t == n_half - 2:
            send_units(i, units // 2, units)
    combine(order[-1][0])
    send_units(order[-1][0], 0, units)
    late = [i for t, (i, j) in enumerate(order) if j == 1 and t >= n_half - 4]
    for i in late[:-1]:
        sum_units(i)
    finish_w_out(tiles // 2, tiles)
    sum_units(late[-1])

    @pl.loop(0, tiles)
    def _(m):
        cols = pl.ds(pl.multiple_of(m * tile, tile), tile)
        o_w_in[cols, :] = dot_tn(xa[:, :, cols].reshape(n_half * 2 * hr, tile), dpa[...])

    slot, gate_slot = [], []
    for i in range(1, nzh):
        wait_for(zr.at[i], zc_r.at[i])
    for e in range(WINDOW):
        total = own[e]
        for i in range(1, nzh):
            total = total + zr[i, e].astype(F32)
        slot.append(jnp.concatenate([total[:CAP, :fh], total[CAP:, :fh]], axis=1))
        gate = jnp.where(
            lax.broadcasted_iota(jnp.int32, (CAP, LANES), 1) == me, total[:CAP, fh:] + total[CAP:, fh:], 0.0
        )
        gate_slot.append(jnp.broadcast_to(jnp.sum(gate, axis=1, keepdims=True), (CAP, LANES)))
    slot = jnp.concatenate(slot, axis=0)
    high = slot.astype(BF).astype(F32)
    middle = (slot - high).astype(BF).astype(F32)
    o_tokens[...] = dot_tn(hot, jnp.concatenate([high, middle, slot - high - middle], axis=0).astype(BF)).astype(BF)
    gate_slot = jnp.concatenate(gate_slot, axis=0)
    gate_slot = jnp.concatenate([gate_slot] * (tok // LANES), axis=1) * hot_f[: WINDOW * CAP]
    for k, r in enumerate((r0, r1)):
        kept = jnp.where(r == expert_of[: WINDOW * CAP], gate_slot, 0.0)
        o_gates[k : k + 1, :] = jnp.sum(kept, axis=0, keepdims=True)

    for i in range(1, nzh):
        wait_for(zs.at[i], zc_s.at[i])
    for i in range(1, nzh):
        for e in range(WINDOW):
            wait_for(zbuf.at[i, e], z_s.at[i, e])
    for i in range(nzh):
        wait_for(rows.at[i, 0, pl.ds(0, units - 1)], xy_s.at[i])
        wait_for(rows.at[i, 0], sib_s.at[i])
        wait_for(cs.at[i, pl.ds(0, units - 1)], c_s.at[i])
        for h in range(2):
            wait_for(res_sib.at[i, h], ds_s.at[i, h])
    wait_for(w_sib, w_s)
    for h in range(2):

        @pl.when(pos[h] < nzl - 1)
        def _():
            wait_for(rs_out.at[h], rs_s.at[h])

        @pl.when(pos[h] > 0)
        def _():
            wait_for(res.at[h], ag_s.at[h])


def body(dims, tokens, grad_out, routes, gates, w_in, w_out):
    nx, nzh, ny, nzl = dims
    units = nx * ny
    hr = units * CAP // 2
    n_half = 2 * nzh
    tok, fe = tokens.shape
    hid = w_in.shape[1]
    all_rows = n_half * 2 * hr
    vmem, hbm = pl.BlockSpec(memory_space=pltpu.VMEM), pl.BlockSpec(memory_space=pltpu.HBM)
    dma = pltpu.SemaphoreType.DMA
    grad_tokens, grad_gates, grad_w_in, grad_w_out = pl.pallas_call(
        functools.partial(kernel, dims),
        out_shape=(
            pltpu.VMEM((tok, fe), BF),
            pltpu.VMEM((2, tok), F32),
            pltpu.VMEM((fe, hid), F32),
            pltpu.VMEM((hid, fe), F32),
        ),
        in_specs=[hbm, hbm, vmem, vmem, hbm, hbm],
        out_specs=(vmem,) * 4,
        scratch_shapes=[
            pltpu.VMEM((tok, fe), BF),
            pltpu.VMEM((tok, fe), BF),
            pltpu.VMEM((fe, hid), BF),
            pltpu.VMEM((hid, fe), BF),
            pltpu.VMEM((nzh, WINDOW, 2 * CAP, fe + LANES), BF),
            pltpu.VMEM((nzh, 2, units, 2 * CAP, fe + LANES), BF),
            pltpu.VMEM((n_half, 2 * hr, fe), BF),
            pltpu.VMEM((n_half, 2 * hr, fe), BF),
            pltpu.VMEM((n_half, 2 * hr, 2 * hid), F32),
            pltpu.VMEM((2, n_half, hr, 3 * hid), BF),
            pltpu.VMEM((2, n_half, hr, 3 * hid), BF),
            pltpu.VMEM((2, n_half, 2 * hr + 16, hid), BF),
            pltpu.VMEM((nzh, 2, 2 * hr + 16, hid), BF),
            pltpu.VMEM((fe, hid), BF),
            pltpu.VMEM((all_rows, hid), BF),
            pltpu.VMEM((all_rows, hid), BF),
            pltpu.VMEM((nzh, units, 2 * CAP, fe // 2 + LANES), BF),
            pltpu.VMEM((nzh, units, 2 * CAP, fe // 2 + LANES), BF),
            pltpu.VMEM((nzh, WINDOW, 2 * CAP, fe // 2 + LANES), BF),
            pltpu.VMEM((nzh, WINDOW, 2 * CAP, fe // 2 + LANES), BF),
            pltpu.VMEM((WINDOW, 2 * CAP, fe // 2 + LANES), F32),
            dma((nzh, WINDOW)), dma((nzh, WINDOW)),
            dma((nzh,)), dma((nzh,)),
            dma((nzh,)), dma((nzh,)),
            dma((2,)), dma((2, n_half)),
            dma((2,)), dma((2, n_half)),
            dma((nzh, 2)), dma((nzh, 2)),
            dma((nzh,)), dma((nzh,)),
            dma((nzh,)), dma((nzh,)),
            dma, dma,
            dma((4,)),
        ],
        compiler_params=pltpu.CompilerParams(
            collective_id=0, has_side_effects=True, vmem_limit_bytes=58 * 1024 * 1024
        ),
    )(tokens, grad_out, routes.T, gates.T, w_in, w_out)
    return grad_tokens, grad_gates.T, grad_w_in, grad_w_out


def solution(mesh):
    dims = (X_CHIPS, ZH_CHIPS, mesh.shape["local"] // 2, mesh.shape["edata"])
    in_specs = (
        P(("node", "local"), "edata"),
        P(("node", "local"), "edata"),
        P(("node", "local"), None),
        P(("node", "local"), None),
        P("edata", ("node", "local")),
        P(("node", "local"), "edata"),
    )
    out_specs = (
        P(("node", "local"), "edata"),
        P(("node", "local"), None),
        P("edata", ("node", "local")),
        P(("node", "local"), "edata"),
    )
    return jax.shard_map(
        functools.partial(body, dims), mesh=mesh, in_specs=in_specs, out_specs=out_specs, check_vma=False
    )
```
